256 devices in a mesh: replica: 4 (over x), shard: 64 (over y, z, core).
Axes of the slice: x: 4, y: 4, z: 8, core: 2. Of those that a mesh axis runs over, the one named last changes fastest.
Arguments:
- grads: bfloat16 [4, 32768, 2048], P('replica', 'shard'), may hold values from -3 to 3
- block_owner: int32 [256], replicated, may hold values from 0 to 511, as said below
- block_offsets: int32 [256, 2], replicated, may hold values from 0 to 32256, as said below
- stat_left: float32 [512, 512, 512], P(('replica', 'shard'))
- stat_right: float32 [512, 512, 512], P(('replica', 'shard'))
- root_left: bfloat16 [512, 512, 512], P(('replica', 'shard'))
- root_right: bfloat16 [512, 512, 512], P(('replica', 'shard'))
Outputs:
- new_left: float32 [512, 512, 512], P(('replica', 'shard'))
- new_right: float32 [512, 512, 512], P(('replica', 'shard'))
- direction: bfloat16 [32768, 2048], P('shard', 'replica')
The draws below stay inside these ranges and needn't reach their ends.
Inputs may be any that keep to these rules, and one draw needn't show every extreme that they name: `block_owner`: values are distinct; value // 2 is the owning device, replica index times 64 plus shard index, and value % 2 its slot; some owner holds 2 blocks in every draw; the first slot of the first device and the last slot of the last device are used in every draw. `block_offsets`: multiples of 512; the blocks cover the window of 32768 x 2048 once.
All inputs are finite; a program needn't handle non-finite values.
Results may differ from the reference program's by a relative error of at most 0.017.
Values may be sent and summed in bfloat16 or wider, within the bound.
No kernel may reach another device: no remote copies, remote signals or barrier semaphores. Data moves between devices by JAX's collectives and lax.ppermute only.
A program may use at most 128 MiB of HBM per device.

```python
import math
import jax
import jax.numpy as jnp
from jax import lax

B = 512
NBC = 4
SLOTS = 2
ROWS = 32768
COLS = 2048
BLOCKS = 256
N_REPLICA = 4
DEVICES = 256


def draw_statistic(key, count):
    first, second = jax.random.split(key)
    noise = jax.random.normal(first, (count, B, B), jnp.float32) * (0.07 / math.sqrt(B))
    diag = jax.random.uniform(second, (count, B), jnp.float32, 0.5, 2.0)
    sym = noise + jnp.swapaxes(noise, 1, 2)
    return sym + diag[:, :, None] * jnp.eye(B, dtype=jnp.float32)[None, :, :]


def draw_root(key, count):
    first, second = jax.random.split(key)
    noise = jax.random.normal(first, (count, B, B), jnp.float32) * (0.5 / math.sqrt(B))
    diag = jax.random.uniform(second, (count, B), jnp.float32, 0.8, 1.25)
    return (noise + diag[:, :, None] * jnp.eye(B, dtype=jnp.float32)[None, :, :]).astype(jnp.bfloat16)


def draw_stat_left(key, part):
    key = jax.random.fold_in(key, 11)
    return draw_statistic(key, DEVICES * SLOTS)


def draw_stat_right(key, part):
    key = jax.random.fold_in(key, 12)
    return draw_statistic(key, DEVICES * SLOTS)


def draw_root_left(key, part):
    key = jax.random.fold_in(key, 13)
    return draw_root(key, DEVICES * SLOTS)


def draw_root_right(key, part):
    key = jax.random.fold_in(key, 14)
    return draw_root(key, DEVICES * SLOTS)


def draw_block_owner(key, part):
    key = jax.random.fold_in(key, 21)
    first, second, third = jax.random.split(key, 3)
    middle = (jax.random.permutation(first, DEVICES - 2) + 1).astype(jnp.int32)
    ends = jnp.array([0, DEVICES - 1], dtype=jnp.int32)
    owners = jnp.concatenate([ends, middle])
    full_count = BLOCKS // (2 * SLOTS)
    single_count = BLOCKS - full_count * SLOTS
    full = owners[:full_count]
    full_values = (full[:, None] * SLOTS + jnp.arange(SLOTS, dtype=jnp.int32)[None, :]).reshape(-1)
    singles = owners[full_count:full_count + single_count]
    single_slot = jax.random.randint(second, (single_count,), 0, SLOTS, dtype=jnp.int32)
    values = jnp.concatenate([full_values, singles * SLOTS + single_slot])
    order = jax.random.permutation(third, BLOCKS).astype(jnp.int32)
    return values[order]


def draw_block_offsets(key, part):
    key = jax.random.fold_in(key, 22)
    order = jax.random.permutation(key, BLOCKS).astype(jnp.int32)
    rows = order // NBC * B
    cols = order % NBC * B
    return jnp.stack([rows, cols], axis=1)


def levels(key, shape, pieces, least, high):
    level, own = 1.0, jax.random.fold_in(key, 6)
    for position, parts in pieces:
        steps = jnp.exp(jax.random.uniform(jax.random.fold_in(own, position), (parts,), jnp.float32, least / len(pieces), high / len(pieces)))
        level = level * jnp.repeat(steps, shape[position] // parts).reshape([-1 if axis == position else 1 for axis in range(len(shape))])
    return level


def normal_values(rng, shape, width, limit, pieces=(), held_as=jnp.bfloat16):
    drawn = width * jax.random.normal(rng, shape, jnp.float32)
    if pieces:
        drawn = drawn * levels(rng, shape, pieces, -0.22, 0.18)
    return jnp.clip(drawn, -limit, limit).astype(held_as)


def setup_inputs(seed: int = 0) -> dict:
    splits = jax.random.split(jax.random.key(seed), 8)
    grads = normal_values(splits[0], (N_REPLICA, ROWS, COLS), 0.5, 3.0, ((0, 4), (1, 64)))
    block_owner = draw_block_owner(jax.random.fold_in(splits[7], 71), 0)
    block_offsets = draw_block_offsets(jax.random.fold_in(splits[7], 71), 0)
    stat_left = draw_stat_left(jax.random.fold_in(splits[7], 71), 0)
    stat_right = draw_stat_right(jax.random.fold_in(splits[7], 71), 0)
    root_left = draw_root_left(jax.random.fold_in(splits[7], 71), 0)
    root_right = draw_root_right(jax.random.fold_in(splits[7], 71), 0)
    return dict(grads=grads, block_owner=block_owner, block_offsets=block_offsets, stat_left=stat_left, stat_right=stat_right, root_left=root_left, root_right=root_right)


def reference(grads, block_owner, block_offsets, stat_left, stat_right, root_left, root_right):
    total = jnp.sum(grads.astype(jnp.float32), axis=0).astype(jnp.bfloat16)
    direction = jnp.zeros((ROWS, COLS), jnp.bfloat16)

    def update(index, carry):
        left_all, right_all, steer_all = carry
        row = block_offsets[index, 0].astype(jnp.int32)
        col = block_offsets[index, 1].astype(jnp.int32)
        owner = block_owner[index].astype(jnp.int32)
        block = lax.dynamic_slice(total, (row, col), (B, B)).astype(jnp.float32)
        gram_left = jnp.dot(block, block.T, precision=lax.Precision.HIGHEST)
        gram_right = jnp.dot(block.T, block, precision=lax.Precision.HIGHEST)
        left_all = left_all.at[owner].add(gram_left / B)
        right_all = right_all.at[owner].add(gram_right / B)
        right_side = jnp.dot(block, root_right[owner].astype(jnp.float32), precision=lax.Precision.HIGHEST).astype(jnp.bfloat16)
        steer = jnp.dot(root_left[owner].astype(jnp.float32), right_side.astype(jnp.float32), precision=lax.Precision.HIGHEST).astype(jnp.bfloat16)
        steer_all = lax.dynamic_update_slice(steer_all, steer, (row, col))
        return left_all, right_all, steer_all

    new_left, new_right, direction = lax.fori_loop(0, BLOCKS, update, (stat_left, stat_right, direction))
    return new_left, new_right, direction
```

```python
import functools

import jax
import jax.numpy as jnp
from jax import lax
from jax.experimental import pallas as pl
from jax.experimental.pallas import tpu as pltpu
from jax.sharding import PartitionSpec as P

ROWS = 8
LANES = 128
UNROLL = 8
VMEM_LIMIT = 48 * 1024 * 1024


def combine_kernel(ncols, me_ref, own_ref, *refs):
    out_ref = refs[-1]
    right_plain, right_sum, left_plain, left_sum = refs[:-1]
    half = right_plain.shape[0]
    across = out_ref.shape[1]
    for side, (first, second) in enumerate(((right_sum, left_plain), (right_plain, left_sum))):
        rows = pl.ds(side * half, half)
        total = (
            own_ref[0, rows, :].astype(jnp.float32)
            + first[...].astype(jnp.float32)
            + second[...].astype(jnp.float32)
        ).astype(out_ref.dtype)
        groups = half // ROWS
        for block in range(ncols):
            for tile in range(across):
                lane = (block * across + tile) * LANES
                piece = total[:, lane : lane + LANES].reshape(groups, ROWS, LANES)
                out_ref[side * groups : (side + 1) * groups, tile, block] = piece


def combine(me, grads, right_plain, right_sum, left_plain, left_sum, ncols):
    replicas, rows, cols = grads.shape
    across = cols // ncols // LANES
    whole = lambda array: pl.BlockSpec(array.shape, lambda step, me_ref: (0,) * array.ndim)
    parts = (right_plain, right_sum, left_plain, left_sum)
    shape = (rows // ROWS, across, ncols, ROWS, LANES)
    return pl.pallas_call(
        functools.partial(combine_kernel, ncols),
        out_shape=jax.ShapeDtypeStruct(shape, grads.dtype),
        grid_spec=pltpu.PrefetchScalarGridSpec(
            num_scalar_prefetch=1,
            grid=(1,),
            in_specs=[
                pl.BlockSpec((1, rows, cols), lambda step, me_ref: (me_ref[0], 0, 0)),
                *[whole(part) for part in parts],
            ],
            out_specs=pl.BlockSpec(shape, lambda step, me_ref: (0,) * len(shape)),
        ),
        compiler_params=pltpu.CompilerParams(vmem_limit_bytes=VMEM_LIMIT),
        name="combine",
    )(me, grads, *parts)


def place_kernel(zero, source_ref, target_ref, in_ref, out_ref):
    if zero:
        out_ref[...] = jnp.zeros_like(out_ref)

    def step(group, carry):
        for offset in range(UNROLL):
            index = group * UNROLL + offset
            out_ref[target_ref[index]] = in_ref[source_ref[index]]
        return carry

    lax.fori_loop(0, source_ref.shape[0] // UNROLL, step, 0)


def place(source, target, tiles, count, zero):
    shape = (count,) + tiles.shape[1:]
    return pl.pallas_call(
        functools.partial(place_kernel, zero),
        out_shape=jax.ShapeDtypeStruct(shape, tiles.dtype),
        grid_spec=pltpu.PrefetchScalarGridSpec(
            num_scalar_prefetch=2,
            grid=(1,),
            in_specs=[pl.BlockSpec(tiles.shape, lambda step, *refs: (0, 0, 0))],
            out_specs=pl.BlockSpec(shape, lambda step, *refs: (0, 0, 0)),
        ),
        compiler_params=pltpu.CompilerParams(vmem_limit_bytes=VMEM_LIMIT),
        name="place",
    )(source, target, tiles)


def assemble(tiles_ref):
    groups, across = tiles_ref.shape[:2]
    columns = [tiles_ref[:, tile, 0].reshape(groups * ROWS, LANES) for tile in range(across)]
    return jnp.concatenate(columns, axis=1)


def steer_kernel(tiles_ref, left_ref, right_ref, out_ref):
    block = assemble(tiles_ref)
    right_side = jnp.dot(block, right_ref[0], preferred_element_type=jnp.float32).astype(
        out_ref.dtype
    )
    steer = jnp.dot(left_ref[0], right_side, preferred_element_type=jnp.float32).astype(
        out_ref.dtype
    )
    groups, across = out_ref.shape[:2]
    for tile in range(across):
        out_ref[:, tile, 0] = steer[:, tile * LANES : (tile + 1) * LANES].reshape(
            groups, ROWS, LANES
        )


def gram_kernel(tiles_ref, left_ref, right_ref, new_left_ref, new_right_ref):
    block = assemble(tiles_ref)
    width = block.shape[0]
    gram_left = lax.dot_general(
        block, block, (((1,), (1,)), ((), ())), preferred_element_type=jnp.float32
    )
    new_left_ref[0] = left_ref[0] + gram_left / width
    gram_right = lax.dot_general(
        block, block, (((0,), (0,)), ((), ())), preferred_element_type=jnp.float32
    )
    new_right_ref[0] = right_ref[0] + gram_right / width


def slot_specs(tiles, square):
    groups, across = tiles.shape[:2]
    return (
        pl.BlockSpec((groups, across, 1, ROWS, LANES), lambda slot: (0, 0, slot, 0, 0)),
        pl.BlockSpec((1, square, square), lambda slot: (slot, 0, 0)),
    )


def steer_slots(tiles, root_left, root_right):
    slots, width = root_left.shape[:2]
    tiled, square = slot_specs(tiles, width)
    return pl.pallas_call(
        steer_kernel,
        out_shape=jax.ShapeDtypeStruct(tiles.shape, tiles.dtype),
        grid=(slots,),
        in_specs=[tiled, square, square],
        out_specs=tiled,
        compiler_params=pltpu.CompilerParams(vmem_limit_bytes=VMEM_LIMIT),
        cost_estimate=pl.CostEstimate(
            flops=4 * slots * width**3, bytes_accessed=8 * slots * width**2, transcendentals=0
        ),
        name="steer",
    )(tiles, root_left, root_right)


def gram_slots(tiles, stat_left, stat_right):
    slots, width = stat_left.shape[:2]
    tiled, square = slot_specs(tiles, width)
    return pl.pallas_call(
        gram_kernel,
        out_shape=[jax.ShapeDtypeStruct(stat.shape, stat.dtype) for stat in (stat_left, stat_right)],
        grid=(slots,),
        in_specs=[tiled, square, square],
        out_specs=[square, square],
        compiler_params=pltpu.CompilerParams(vmem_limit_bytes=VMEM_LIMIT),
        cost_estimate=pl.CostEstimate(
            flops=4 * slots * width**3, bytes_accessed=18 * slots * width**2, transcendentals=0
        ),
        name="gram",
    )(tiles, stat_left, stat_right)


def reduce_rows(grads, replicas, ncols):
    rows, cols = grads.shape[1] // replicas, grads.shape[2]
    parts = grads.reshape(replicas, 2, rows // 2, cols)
    me = lax.axis_index("replica")
    rightward = [(i, (i + 1) % replicas) for i in range(replicas)]
    leftward = [(i, (i - 1) % replicas) for i in range(replicas)]

    def part(shift, side):
        index = lax.rem(me + shift, replicas)
        return lax.dynamic_slice(parts, (index, side, 0, 0), (1, 1, rows // 2, cols))[0, 0]

    from_left = lax.ppermute(part(2, 0), "replica", rightward)
    from_right = lax.ppermute(part(2, 1), "replica", leftward)
    right_plain = lax.ppermute(part(1, 1), "replica", rightward)
    left_plain = lax.ppermute(part(3, 0), "replica", leftward)

    def add(first, second):
        return (first.astype(jnp.float32) + second.astype(jnp.float32)).astype(grads.dtype)

    right_sum = lax.ppermute(add(part(1, 0), from_left), "replica", rightward)
    left_sum = lax.ppermute(add(part(3, 1), from_right), "replica", leftward)
    return combine(
        jnp.reshape(me, (1,)).astype(jnp.int32),
        grads.reshape(replicas, rows, cols),
        right_plain,
        right_sum,
        left_plain,
        left_sum,
        ncols,
    )


def on_device(grads, block_owner, block_offsets, stat_left, stat_right, root_left, root_right):
    shards = lax.axis_size("shard")
    replicas = lax.axis_size("replica")
    devices = replicas * shards
    slots, width = stat_left.shape[:2]
    ncols = grads.shape[2] // width
    blocks = block_owner.shape[0]
    across = width // LANES
    groups = width // ROWS
    row = block_offsets[:, 0] // width
    col = block_offsets[:, 1] // width

    summed = reduce_rows(grads, replicas, ncols)
    spread = lax.all_to_all(
        summed.reshape(shards, ncols, ROWS, LANES), "shard", split_axis=0, concat_axis=0, tiled=True
    )
    by_slot = place(
        row * ncols + col, block_owner, spread.reshape(blocks, ROWS, LANES), devices * slots, True
    )
    everyone = ("replica", "shard")
    owned = lax.all_to_all(
        by_slot.reshape(devices, slots, ROWS, LANES),
        everyone,
        split_axis=0,
        concat_axis=0,
        tiled=True,
    ).reshape(groups, across, slots, ROWS, LANES)
    steer = steer_slots(owned, root_left, root_right)
    new_left, new_right = gram_slots(owned, stat_left, stat_right)
    returned = lax.all_to_all(
        steer.reshape(devices, slots, ROWS, LANES),
        everyone,
        split_axis=0,
        concat_axis=0,
        tiled=True,
    )
    by_place = place(
        block_owner,
        col * shards + row,
        returned.reshape(devices * slots, ROWS, LANES),
        blocks,
        False,
    )
    home = lax.all_to_all(by_place, everyone, split_axis=0, concat_axis=0, tiled=True)
    direction = (
        home.reshape(groups, across, ROWS, LANES).transpose(0, 2, 1, 3).reshape(width, width)
    )
    return (new_left, new_right, direction)


def solution(mesh):
    placed = (
        P("replica", "shard", None),
        P(),
        P(),
        P(("replica", "shard"), None, None),
        P(("replica", "shard"), None, None),
        P(("replica", "shard"), None, None),
        P(("replica", "shard"), None, None),
    )
    return jax.shard_map(
        on_device,
        mesh=mesh,
        in_specs=placed,
        out_specs=(
            P(("replica", "shard"), None, None),
            P(("replica", "shard"), None, None),
            P("shard", "replica"),
        ),
        check_vma=False,
    )
```

```python
import functools

import jax
import jax.numpy as jnp
from jax import lax
from jax.experimental import pallas as pl
from jax.experimental.pallas import tpu as pltpu
from jax.sharding import PartitionSpec as P

ROWS = 8
LANES = 128
UNROLL = 16
PARTS = 4
VMEM_LIMIT = 16 * 1024 * 1024
GRAM_VMEM = 62 * 1024 * 1024
IN_VMEM = pl.BlockSpec(memory_space=pltpu.VMEM)
IN_SMEM = pl.BlockSpec(memory_space=pltpu.SMEM)
PARAMS = pltpu.CompilerParams(vmem_limit_bytes=VMEM_LIMIT)


def combine_kernel(ncols, me_ref, own_ref, *refs):
    out_ref = refs[-1]
    right_plain, right_sum, left_plain, left_sum = refs[:-1]
    half = right_plain.shape[0]
    across = out_ref.shape[1]
    groups = half // ROWS
    me = me_ref[0]
    for side, (first, second) in enumerate(((right_sum, left_plain), (right_plain, left_sum))):
        for block in range(ncols):
            for tile in range(across):
                lanes = pl.ds((block * across + tile) * LANES, LANES)
                total = (
                    own_ref[me, side, :, lanes].astype(jnp.float32)
                    + first[:, lanes].astype(jnp.float32)
                    + second[:, lanes].astype(jnp.float32)
                ).astype(out_ref.dtype)
                rows = pl.ds(side * groups, groups)
                out_ref[rows, tile, block] = total.reshape(groups, ROWS, LANES)


def combine(me, parts, right_plain, right_sum, left_plain, left_sum, ncols):
    half, cols = right_plain.shape
    shape = (2 * half // ROWS, cols // ncols // LANES, ncols, ROWS, LANES)
    return pl.pallas_call(
        functools.partial(combine_kernel, ncols),
        out_shape=jax.ShapeDtypeStruct(shape, parts.dtype),
        in_specs=[IN_SMEM] + [IN_VMEM] * 5,
        out_specs=IN_VMEM,
        compiler_params=PARAMS,
        name="combine",
    )(me, parts, right_plain, right_sum, left_plain, left_sum)


def place_rows(source_ref, target_ref, in_ref, out_ref, begin, count):
    def step(group, carry):
        rows = [begin + group * UNROLL + offset for offset in range(UNROLL)]
        pieces = [in_ref[source_ref[row]] for row in rows]
        for row, piece in zip(rows, pieces):
            out_ref[target_ref[row]] = piece
        return carry

    lax.fori_loop(0, count // UNROLL, step, 0)


def to_slots_kernel(source_ref, target_ref, in_ref, out_ref):
    out_ref[...] = jnp.zeros_like(out_ref)
    place_rows(source_ref, target_ref, in_ref, out_ref, 0, source_ref.shape[0])


def to_slots(source, target, tiles, count):
    return pl.pallas_call(
        to_slots_kernel,
        out_shape=jax.ShapeDtypeStruct((count,) + tiles.shape[1:], tiles.dtype),
        in_specs=[IN_SMEM, IN_SMEM, IN_VMEM],
        out_specs=IN_VMEM,
        compiler_params=PARAMS,
        name="to_slots",
    )(source, target, tiles)


def pick_kernel(index_ref, in_ref, out_ref, filled, sems):
    parts = sems.shape[0]
    count = filled.shape[0] // parts

    def move(part):
        rows = pl.ds(part * count, count)
        return pltpu.make_async_copy(filled.at[rows], out_ref.at[rows], sems.at[part])

    for part in range(parts):

        def step(group, carry):
            rows = [part * count + group * UNROLL + offset for offset in range(UNROLL)]
            pieces = [in_ref[index_ref[row]] for row in rows]
            for row, piece in zip(rows, pieces):
                filled[row] = piece
            return carry

        lax.fori_loop(0, count // UNROLL, step, 0)
        move(part).start()
    for part in range(parts):
        move(part).wait()


def pick(index, tiles):
    shape = index.shape + tiles.shape[1:]
    return pl.pallas_call(
        pick_kernel,
        out_shape=jax.ShapeDtypeStruct(shape, tiles.dtype),
        in_specs=[IN_SMEM, IN_VMEM],
        out_specs=pl.BlockSpec(memory_space=pltpu.HBM),
        scratch_shapes=[pltpu.VMEM(shape, tiles.dtype), pltpu.SemaphoreType.DMA((PARTS,))],
        compiler_params=PARAMS,
        name="pick",
    )(index, tiles)


def assemble(tiles_ref, slot):
    groups, across = tiles_ref.shape[:2]
    columns = [tiles_ref[:, tile, slot].reshape(groups * ROWS, LANES) for tile in range(across)]
    return jnp.concatenate(columns, axis=1)


def steer_kernel(tiles_ref, left_ref, right_ref, out_ref):
    groups, across, slots = out_ref.shape[:3]
    for slot in range(slots):
        block = assemble(tiles_ref, slot)
        right_side = jnp.dot(block, right_ref[slot], preferred_element_type=jnp.float32)
        right_side = right_side.astype(out_ref.dtype)
        steer = jnp.dot(left_ref[slot], right_side, preferred_element_type=jnp.float32)
        steer = steer.astype(out_ref.dtype)
        for tile in range(across):
            piece = steer[:, tile * LANES : (tile + 1) * LANES]
            out_ref[:, tile, slot] = piece.reshape(groups, ROWS, LANES)


def gram_kernel(tiles_ref, left_ref, right_ref, new_left_ref, new_right_ref, held, in_sems, out_sems):
    slots, width = left_ref.shape[:2]

    def copies(slot):
        for side, (old, new) in enumerate(((left_ref, new_left_ref), (right_ref, new_right_ref))):
            space = held.at[slot, side]
            yield (
                pltpu.make_async_copy(old.at[slot], space, in_sems.at[slot, side]),
                pltpu.make_async_copy(space, new.at[slot], out_sems.at[slot, side]),
            )

    for slot in range(slots):
        for arriving, _ in copies(slot):
            arriving.start()
    for slot in range(slots):
        block = assemble(tiles_ref, slot)
        for side, (arriving, leaving) in enumerate(copies(slot)):
            contracted = ((1 - side,), (1 - side,))
            gram = lax.dot_general(
                block, block, (contracted, ((), ())), preferred_element_type=jnp.float32
            )
            arriving.wait()
            held[slot, side] += gram / width
            leaving.start()
    for slot in range(slots):
        for _, leaving in copies(slot):
            leaving.wait()


def steer_slots(tiles, root_left, root_right):
    slots, width = root_left.shape[:2]
    return pl.pallas_call(
        steer_kernel,
        out_shape=jax.ShapeDtypeStruct(tiles.shape, tiles.dtype),
        in_specs=[IN_VMEM] * 3,
        out_specs=IN_VMEM,
        compiler_params=PARAMS,
        cost_estimate=pl.CostEstimate(
            flops=4 * slots * width**3, bytes_accessed=8 * slots * width**2, transcendentals=0
        ),
        name="steer",
    )(tiles, root_left, root_right)


def gram_slots(tiles, stat_left, stat_right):
    slots, width = stat_left.shape[:2]
    in_hbm = pl.BlockSpec(memory_space=pltpu.HBM)
    return pl.pallas_call(
        gram_kernel,
        out_shape=[jax.ShapeDtypeStruct(stat.shape, stat.dtype) for stat in (stat_left, stat_right)],
        in_specs=[IN_VMEM, in_hbm, in_hbm],
        out_specs=[in_hbm, in_hbm],
        scratch_shapes=[
            pltpu.VMEM((slots, 2, width, width), jnp.float32),
            pltpu.SemaphoreType.DMA((slots, 2)),
            pltpu.SemaphoreType.DMA((slots, 2)),
        ],
        compiler_params=pltpu.CompilerParams(vmem_limit_bytes=GRAM_VMEM),
        cost_estimate=pl.CostEstimate(
            flops=4 * slots * width**3, bytes_accessed=18 * slots * width**2, transcendentals=0
        ),
        name="gram",
    )(tiles, stat_left, stat_right)


def reduce_rows(grads, replicas, ncols):
    rows, cols = grads.shape[1] // replicas, grads.shape[2]
    parts = grads.reshape(replicas, 2, rows // 2, cols)
    me = lax.axis_index("replica")
    rightward = [(i, (i + 1) % replicas) for i in range(replicas)]
    leftward = [(i, (i - 1) % replicas) for i in range(replicas)]

    def part(shift, side):
        index = lax.rem(me + shift, replicas)
        return lax.dynamic_slice(parts, (index, side, 0, 0), (1, 1, rows // 2, cols))[0, 0]

    parts, far_right, far_left = lax.optimization_barrier((parts, part(2, 0), part(2, 1)))
    from_left = lax.ppermute(far_right, "replica", rightward)
    from_right = lax.ppermute(far_left, "replica", leftward)
    right_plain = lax.ppermute(part(1, 1), "replica", rightward)
    left_plain = lax.ppermute(part(3, 0), "replica", leftward)

    def add(first, second):
        return (first.astype(jnp.float32) + second.astype(jnp.float32)).astype(grads.dtype)

    right_sum = lax.ppermute(add(part(1, 0), from_left), "replica", rightward)
    left_sum = lax.ppermute(add(part(3, 1), from_right), "replica", leftward)
    return combine(
        jnp.reshape(me, (1,)).astype(jnp.int32),
        parts,
        right_plain,
        right_sum,
        left_plain,
        left_sum,
        ncols,
    )


def on_device(grads, block_owner, block_offsets, stat_left, stat_right, root_left, root_right):
    shards = lax.axis_size("shard")
    replicas = lax.axis_size("replica")
    devices = replicas * shards
    slots, width = stat_left.shape[:2]
    ncols = grads.shape[2] // width
    blocks = block_owner.shape[0]
    across = width // LANES
    groups = width // ROWS
    row = block_offsets[:, 0] // width
    col = block_offsets[:, 1] // width

    here = (col * shards + row)[None, :] == jnp.arange(blocks, dtype=jnp.int32)[:, None]
    owner_of = jnp.sum(jnp.where(here, block_owner[None, :], 0), axis=1)

    summed = reduce_rows(grads, replicas, ncols)
    summed, owner_of, source = lax.optimization_barrier((summed, owner_of, row * ncols + col))
    spread = lax.all_to_all(
        summed.reshape(shards, ncols, ROWS, LANES), "shard", split_axis=0, concat_axis=0, tiled=True
    )
    by_slot = to_slots(
        source, block_owner, spread.reshape(blocks, ROWS, LANES), devices * slots
    )
    everyone = ("replica", "shard")
    owned = lax.all_to_all(
        by_slot.reshape(devices, slots, ROWS, LANES),
        everyone,
        split_axis=0,
        concat_axis=0,
        tiled=True,
    ).reshape(groups, across, slots, ROWS, LANES)
    steer = steer_slots(owned, root_left, root_right)
    new_left, new_right = gram_slots(owned, stat_left, stat_right)
    returned = lax.all_to_all(
        steer.reshape(devices, slots, ROWS, LANES),
        everyone,
        split_axis=0,
        concat_axis=0,
        tiled=True,
    )
    by_place = pick(owner_of, returned.reshape(devices * slots, ROWS, LANES))
    home = lax.all_to_all(by_place, everyone, split_axis=0, concat_axis=0, tiled=True)
    direction = (
        home.reshape(groups, across, ROWS, LANES).transpose(0, 2, 1, 3).reshape(width, width)
    )
    return (new_left, new_right, direction)


def solution(mesh):
    placed = (
        P("replica", "shard", None),
        P(),
        P(),
        P(("replica", "shard"), None, None),
        P(("replica", "shard"), None, None),
        P(("replica", "shard"), None, None),
        P(("replica", "shard"), None, None),
    )
    return jax.shard_map(
        on_device,
        mesh=mesh,
        in_specs=placed,
        out_specs=(
            P(("replica", "shard"), None, None),
            P(("replica", "shard"), None, None),
            P("shard", "replica"),
        ),
        check_vma=False,
    )
```

```python
import functools

import jax
import jax.numpy as jnp
from jax import lax
from jax.experimental import pallas as pl
from jax.experimental.pallas import tpu as pltpu
from jax.sharding import PartitionSpec as P

ROWS = 8
LANES = 128
UNROLL = 16
PARTS = 4
FAR_SHARD = 40
FAR_DEVICE = 168
STRIDE = 2
VMEM_LIMIT = 16 * 1024 * 1024
GRAM_VMEM = 62 * 1024 * 1024
IN_VMEM = pl.BlockSpec(memory_space=pltpu.VMEM)
IN_SMEM = pl.BlockSpec(memory_space=pltpu.SMEM)
PARAMS = pltpu.CompilerParams(vmem_limit_bytes=VMEM_LIMIT)


def combine_kernel(ncols, me_ref, own_ref, *refs):
    out_ref = refs[-1]
    right_plain, right_sum, left_plain, left_sum = refs[:-1]
    half = right_plain.shape[0]
    across = out_ref.shape[1]
    groups = half // ROWS
    me = me_ref[0]
    for side, (first, second) in enumerate(((right_sum, left_plain), (right_plain, left_sum))):
        for block in range(ncols):
            for tile in range(across):
                lanes = pl.ds((block * across + tile) * LANES, LANES)
                total = (
                    own_ref[me, side, :, lanes].astype(jnp.float32)
                    + first[:, lanes].astype(jnp.float32)
                    + second[:, lanes].astype(jnp.float32)
                ).astype(out_ref.dtype)
                for group in range(groups):
                    row = (side * groups + group) ^ (FAR_SHARD // across)
                    out_ref[row, tile, block] = total[group * ROWS : (group + 1) * ROWS]


def combine(me, parts, right_plain, right_sum, left_plain, left_sum, ncols):
    half, cols = right_plain.shape
    shape = (2 * half // ROWS, cols // ncols // LANES, ncols, ROWS, LANES)
    return pl.pallas_call(
        functools.partial(combine_kernel, ncols),
        out_shape=jax.ShapeDtypeStruct(shape, parts.dtype),
        in_specs=[IN_SMEM] + [IN_VMEM] * 5,
        out_specs=IN_VMEM,
        compiler_params=PARAMS,
        name="combine",
    )(me, parts, right_plain, right_sum, left_plain, left_sum)


def place_rows(source_ref, target_ref, in_ref, out_ref, begin, count):
    def step(group, carry):
        rows = [begin + group * UNROLL + offset for offset in range(UNROLL)]
        pieces = [in_ref[source_ref[row]] for row in rows]
        for row, piece in zip(rows, pieces):
            out_ref[target_ref[row]] = piece
        return carry

    lax.fori_loop(0, count // UNROLL, step, 0)


def to_slots_kernel(source_ref, target_ref, in_ref, out_ref):
    out_ref[...] = jnp.zeros_like(out_ref)
    place_rows(source_ref, target_ref, in_ref, out_ref, 0, source_ref.shape[0])


def to_slots(source, target, tiles, count):
    return pl.pallas_call(
        to_slots_kernel,
        out_shape=jax.ShapeDtypeStruct((count,) + tiles.shape[1:], tiles.dtype),
        in_specs=[IN_SMEM, IN_SMEM, IN_VMEM],
        out_specs=IN_VMEM,
        compiler_params=PARAMS,
        name="to_slots",
    )(source, target, tiles)


def pick_kernel(index_ref, in_ref, out_ref, filled, sems):
    parts = sems.shape[0]
    count = filled.shape[0] // parts

    def move(part):
        rows = pl.ds(part * count, count)
        return pltpu.make_async_copy(filled.at[rows], out_ref.at[rows], sems.at[part])

    for part in range(parts):

        def step(group, carry):
            rows = [part * count + group * UNROLL + offset for offset in range(UNROLL)]
            pieces = [in_ref[index_ref[row]] for row in rows]
            for row, piece in zip(rows, pieces):
                filled[row] = piece
            return carry

        lax.fori_loop(0, count // UNROLL, step, 0)
        move(part).start()
    for part in range(parts):
        move(part).wait()


def pick(index, tiles):
    shape = index.shape + tiles.shape[1:]
    return pl.pallas_call(
        pick_kernel,
        out_shape=jax.ShapeDtypeStruct(shape, tiles.dtype),
        in_specs=[IN_SMEM, IN_VMEM],
        out_specs=pl.BlockSpec(memory_space=pltpu.HBM),
        scratch_shapes=[pltpu.VMEM(shape, tiles.dtype), pltpu.SemaphoreType.DMA((PARTS,))],
        compiler_params=PARAMS,
        name="pick",
    )(index, tiles)


def assemble(tiles_ref, slot):
    groups, across = tiles_ref.shape[:2]
    columns = [tiles_ref[:, tile, slot].reshape(groups * ROWS, LANES) for tile in range(across)]
    return jnp.concatenate(columns, axis=1)


def steer_kernel(tiles_ref, left_ref, right_ref, out_ref):
    groups, across, slots = out_ref.shape[:3]
    for slot in range(slots):
        block = assemble(tiles_ref, slot)
        right_side = jnp.dot(block, right_ref[slot], preferred_element_type=jnp.float32)
        right_side = right_side.astype(out_ref.dtype)
        steer = jnp.dot(left_ref[slot], right_side, preferred_element_type=jnp.float32)
        steer = steer.astype(out_ref.dtype)
        for tile in range(across):
            piece = steer[:, tile * LANES : (tile + 1) * LANES].reshape(groups, ROWS, LANES)
            for group in range(0, groups, STRIDE):
                rows = pl.ds(group ^ (FAR_DEVICE // across), STRIDE)
                out_ref[rows, tile, slot] = piece[group : group + STRIDE]


def gram_kernel(tiles_ref, left_ref, right_ref, new_left_ref, new_right_ref, held, in_sems, out_sems):
    slots, width = left_ref.shape[:2]

    def copies(slot):
        for side, (old, new) in enumerate(((left_ref, new_left_ref), (right_ref, new_right_ref))):
            space = held.at[slot, side]
            yield (
                pltpu.make_async_copy(old.at[slot], space, in_sems.at[slot, side]),
                pltpu.make_async_copy(space, new.at[slot], out_sems.at[slot, side]),
            )

    for slot in range(slots):
        for arriving, _ in copies(slot):
            arriving.start()
    for slot in range(slots):
        block = assemble(tiles_ref, slot)
        for side, (arriving, leaving) in enumerate(copies(slot)):
            contracted = ((1 - side,), (1 - side,))
            gram = lax.dot_general(
                block, block, (contracted, ((), ())), preferred_element_type=jnp.float32
            )
            arriving.wait()
            held[slot, side] += gram / width
            leaving.start()
    for slot in range(slots):
        for _, leaving in copies(slot):
            leaving.wait()


def steer_slots(tiles, root_left, root_right):
    slots, width = root_left.shape[:2]
    return pl.pallas_call(
        steer_kernel,
        out_shape=jax.ShapeDtypeStruct(tiles.shape, tiles.dtype),
        in_specs=[IN_VMEM] * 3,
        out_specs=IN_VMEM,
        compiler_params=PARAMS,
        cost_estimate=pl.CostEstimate(
            flops=4 * slots * width**3, bytes_accessed=8 * slots * width**2, transcendentals=0
        ),
        name="steer",
    )(tiles, root_left, root_right)


def gram_slots(tiles, stat_left, stat_right):
    slots, width = stat_left.shape[:2]
    in_hbm = pl.BlockSpec(memory_space=pltpu.HBM)
    return pl.pallas_call(
        gram_kernel,
        out_shape=[jax.ShapeDtypeStruct(stat.shape, stat.dtype) for stat in (stat_left, stat_right)],
        in_specs=[IN_VMEM, in_hbm, in_hbm],
        out_specs=[in_hbm, in_hbm],
        scratch_shapes=[
            pltpu.VMEM((slots, 2, width, width), jnp.float32),
            pltpu.SemaphoreType.DMA((slots, 2)),
            pltpu.SemaphoreType.DMA((slots, 2)),
        ],
        compiler_params=pltpu.CompilerParams(vmem_limit_bytes=GRAM_VMEM),
        cost_estimate=pl.CostEstimate(
            flops=4 * slots * width**3, bytes_accessed=18 * slots * width**2, transcendentals=0
        ),
        name="gram",
    )(tiles, stat_left, stat_right)


def reduce_rows(grads, replicas, ncols):
    rows, cols = grads.shape[1] // replicas, grads.shape[2]
    parts = grads.reshape(replicas, 2, rows // 2, cols)
    me = lax.axis_index("replica")
    rightward = [(i, (i + 1) % replicas) for i in range(replicas)]
    leftward = [(i, (i - 1) % replicas) for i in range(replicas)]

    def part(shift, side):
        index = lax.rem(me + shift, replicas)
        return lax.dynamic_slice(parts, (index, side, 0, 0), (1, 1, rows // 2, cols))[0, 0]

    parts, far_right, far_left = lax.optimization_barrier((parts, part(2, 0), part(2, 1)))
    from_left = lax.ppermute(far_right, "replica", rightward)
    from_right = lax.ppermute(far_left, "replica", leftward)
    right_plain = lax.ppermute(part(1, 1), "replica", rightward)
    left_plain = lax.ppermute(part(3, 0), "replica", leftward)

    def add(first, second):
        return (first.astype(jnp.float32) + second.astype(jnp.float32)).astype(grads.dtype)

    right_sum = lax.ppermute(add(part(1, 0), from_left), "replica", rightward)
    left_sum = lax.ppermute(add(part(3, 1), from_right), "replica", leftward)
    return combine(
        jnp.reshape(me, (1,)).astype(jnp.int32),
        parts,
        right_plain,
        right_sum,
        left_plain,
        left_sum,
        ncols,
    )


def on_device(grads, block_owner, block_offsets, stat_left, stat_right, root_left, root_right):
    shards = lax.axis_size("shard")
    replicas = lax.axis_size("replica")
    devices = replicas * shards
    slots, width = stat_left.shape[:2]
    ncols = grads.shape[2] // width
    blocks = block_owner.shape[0]
    across = width // LANES
    groups = width // ROWS
    row = block_offsets[:, 0] // width
    col = block_offsets[:, 1] // width

    target = (col * shards + row) ^ FAR_DEVICE
    here = target[None, :] == jnp.arange(blocks, dtype=jnp.int32)[:, None]
    owner_of = jnp.sum(jnp.where(here, block_owner[None, :], 0), axis=1)

    summed = reduce_rows(grads, replicas, ncols)
    summed, owner_of, source = lax.optimization_barrier(
        (summed, owner_of, (row ^ FAR_SHARD) * ncols + col)
    )
    spread = lax.all_to_all(
        summed.reshape(shards, ncols, ROWS, LANES),
        "shard",
        split_axis=0,
        concat_axis=0,
        axis_index_groups=[[index ^ FAR_SHARD for index in range(shards)]],
        tiled=True,
    )
    by_slot = to_slots(
        source, block_owner, spread.reshape(blocks, ROWS, LANES), devices * slots
    )
    everyone = ("replica", "shard")
    owned = lax.all_to_all(
        by_slot.reshape(devices, slots, ROWS, LANES),
        everyone,
        split_axis=0,
        concat_axis=0,
        tiled=True,
    ).reshape(groups, across, slots, ROWS, LANES)
    steer = steer_slots(owned, root_left, root_right)
    new_left, new_right = gram_slots(owned, stat_left, stat_right)
    returned = lax.all_to_all(
        steer.reshape(devices, slots, ROWS, LANES),
        everyone,
        split_axis=0,
        concat_axis=0,
        tiled=True,
    )
    by_place = pick(owner_of, returned.reshape(devices * slots, ROWS, LANES))
    home = lax.all_to_all(
        by_place,
        everyone,
        split_axis=0,
        concat_axis=0,
        axis_index_groups=[[index ^ FAR_DEVICE for index in range(devices)]],
        tiled=True,
    )
    direction = (
        home.reshape(groups, across, ROWS, LANES).transpose(0, 2, 1, 3).reshape(width, width)
    )
    return (new_left, new_right, direction)


def solution(mesh):
    placed = (
        P("replica", "shard", None),
        P(),
        P(),
        P(("replica", "shard"), None, None),
        P(("replica", "shard"), None, None),
        P(("replica", "shard"), None, None),
        P(("replica", "shard"), None, None),
    )
    return jax.shard_map(
        on_device,
        mesh=mesh,
        in_specs=placed,
        out_specs=(
            P(("replica", "shard"), None, None),
            P(("replica", "shard"), None, None),
            P("shard", "replica"),
        ),
        check_vma=False,
    )
```

```python
import functools

import jax
import jax.numpy as jnp
from jax import lax
from jax.experimental import pallas as pl
from jax.experimental.pallas import tpu as pltpu
from jax.sharding import PartitionSpec as P

ROWS = 8
LANES = 128
UNROLL = 32
PARTS = 4
FAR_SHARD = 40
FAR_DEVICE = 168
STRIDE = 2
VMEM_LIMIT = 16 * 1024 * 1024
GRAM_VMEM = 62 * 1024 * 1024
IN_VMEM = pl.BlockSpec(memory_space=pltpu.VMEM)
IN_SMEM = pl.BlockSpec(memory_space=pltpu.SMEM)
PARAMS = pltpu.CompilerParams(vmem_limit_bytes=VMEM_LIMIT)


def combine_kernel(ncols, me_ref, own_ref, *refs):
    out_ref = refs[-1]
    right_plain, right_sum, left_plain, left_sum = refs[:-1]
    half = right_plain.shape[0]
    across = out_ref.shape[1]
    groups = half // ROWS
    me = me_ref[0]
    for side, (first, second) in enumerate(((right_sum, left_plain), (right_plain, left_sum))):
        for block in range(ncols):
            for tile in range(across):
                lanes = pl.ds((block * across + tile) * LANES, LANES)
                total = (
                    own_ref[me, side, :, lanes].astype(jnp.float32)
                    + first[:, lanes].astype(jnp.float32)
                    + second[:, lanes].astype(jnp.float32)
                ).astype(out_ref.dtype)
                for group in range(groups):
                    row = (side * groups + group) ^ (FAR_SHARD // across)
                    out_ref[row, tile, block] = total[group * ROWS : (group + 1) * ROWS]


def combine(me, parts, right_plain, right_sum, left_plain, left_sum, ncols):
    half, cols = right_plain.shape
    shape = (2 * half // ROWS, cols // ncols // LANES, ncols, ROWS, LANES)
    return pl.pallas_call(
        functools.partial(combine_kernel, ncols),
        out_shape=jax.ShapeDtypeStruct(shape, parts.dtype),
        in_specs=[IN_SMEM] + [IN_VMEM] * 5,
        out_specs=IN_VMEM,
        compiler_params=PARAMS,
        name="combine",
    )(me, parts, right_plain, right_sum, left_plain, left_sum)


def to_slots_kernel(target_ref, in_ref, out_ref):
    out_ref[...] = jnp.zeros_like(out_ref)

    def step(group, carry):
        rows = [group * UNROLL + offset for offset in range(UNROLL)]
        pieces = [in_ref[row] for row in rows]
        for row, piece in zip(rows, pieces):
            out_ref[target_ref[row]] = piece
        return carry

    lax.fori_loop(0, target_ref.shape[0] // UNROLL, step, 0)


def to_slots(target, tiles, count):
    return pl.pallas_call(
        to_slots_kernel,
        out_shape=jax.ShapeDtypeStruct((count,) + tiles.shape[1:], tiles.dtype),
        in_specs=[IN_SMEM, IN_VMEM],
        out_specs=IN_VMEM,
        compiler_params=PARAMS,
        name="to_slots",
    )(target, tiles)


def pick_kernel(index_ref, in_ref, out_ref, filled, sems):
    parts = sems.shape[0]
    count = filled.shape[0] // parts

    def move(part):
        rows = pl.ds(part * count, count)
        return pltpu.make_async_copy(filled.at[rows], out_ref.at[rows], sems.at[part])

    for part in range(parts):

        def step(group, carry):
            rows = [part * count + group * UNROLL + offset for offset in range(UNROLL)]
            pieces = [in_ref[index_ref[row]] for row in rows]
            for row, piece in zip(rows, pieces):
                filled[row] = piece
            return carry

        lax.fori_loop(0, count // UNROLL, step, 0)
        move(part).start()
    for part in range(parts):
        move(part).wait()


def pick(index, tiles):
    shape = index.shape + tiles.shape[1:]
    return pl.pallas_call(
        pick_kernel,
        out_shape=jax.ShapeDtypeStruct(shape, tiles.dtype),
        in_specs=[IN_SMEM, IN_VMEM],
        out_specs=pl.BlockSpec(memory_space=pltpu.HBM),
        scratch_shapes=[pltpu.VMEM(shape, tiles.dtype), pltpu.SemaphoreType.DMA((PARTS,))],
        compiler_params=PARAMS,
        name="pick",
    )(index, tiles)


def assemble(tiles_ref, slot):
    groups, across = tiles_ref.shape[:2]
    columns = [tiles_ref[:, tile, slot].reshape(groups * ROWS, LANES) for tile in range(across)]
    return jnp.concatenate(columns, axis=1)


def steer_kernel(tiles_ref, left_ref, right_ref, out_ref):
    groups, across, slots = out_ref.shape[:3]
    for slot in range(slots):
        block = assemble(tiles_ref, slot)
        right_side = jnp.dot(block, right_ref[slot], preferred_element_type=jnp.float32)
        right_side = right_side.astype(out_ref.dtype)
        steer = jnp.dot(left_ref[slot], right_side, preferred_element_type=jnp.float32)
        steer = steer.astype(out_ref.dtype)
        for tile in range(across):
            piece = steer[:, tile * LANES : (tile + 1) * LANES].reshape(groups, ROWS, LANES)
            for group in range(0, groups, STRIDE):
                rows = pl.ds(group ^ (FAR_DEVICE // across), STRIDE)
                out_ref[rows, tile, slot] = piece[group : group + STRIDE]


def gram_kernel(tiles_ref, left_ref, right_ref, new_left_ref, new_right_ref, held, in_sems, out_sems):
    slots, width = left_ref.shape[:2]

    def copies(slot):
        for side, (old, new) in enumerate(((left_ref, new_left_ref), (right_ref, new_right_ref))):
            space = held.at[slot, side]
            yield (
                pltpu.make_async_copy(old.at[slot], space, in_sems.at[slot, side]),
                pltpu.make_async_copy(space, new.at[slot], out_sems.at[slot, side]),
            )

    for slot in range(slots):
        for arriving, _ in copies(slot):
            arriving.start()
    for slot in range(slots):
        block = assemble(tiles_ref, slot)
        for side, (arriving, leaving) in enumerate(copies(slot)):
            contracted = ((1 - side,), (1 - side,))
            gram = lax.dot_general(
                block, block, (contracted, ((), ())), preferred_element_type=jnp.float32
            )
            arriving.wait()
            held[slot, side] += gram / width
            leaving.start()
    for slot in range(slots):
        for _, leaving in copies(slot):
            leaving.wait()


def steer_slots(tiles, root_left, root_right):
    slots, width = root_left.shape[:2]
    return pl.pallas_call(
        steer_kernel,
        out_shape=jax.ShapeDtypeStruct(tiles.shape, tiles.dtype),
        in_specs=[IN_VMEM] * 3,
        out_specs=IN_VMEM,
        compiler_params=PARAMS,
        cost_estimate=pl.CostEstimate(
            flops=4 * slots * width**3, bytes_accessed=8 * slots * width**2, transcendentals=0
        ),
        name="steer",
    )(tiles, root_left, root_right)


def gram_slots(tiles, stat_left, stat_right):
    slots, width = stat_left.shape[:2]
    in_hbm = pl.BlockSpec(memory_space=pltpu.HBM)
    return pl.pallas_call(
        gram_kernel,
        out_shape=[jax.ShapeDtypeStruct(stat.shape, stat.dtype) for stat in (stat_left, stat_right)],
        in_specs=[IN_VMEM, in_hbm, in_hbm],
        out_specs=[in_hbm, in_hbm],
        scratch_shapes=[
            pltpu.VMEM((slots, 2, width, width), jnp.float32),
            pltpu.SemaphoreType.DMA((slots, 2)),
            pltpu.SemaphoreType.DMA((slots, 2)),
        ],
        compiler_params=pltpu.CompilerParams(vmem_limit_bytes=GRAM_VMEM),
        cost_estimate=pl.CostEstimate(
            flops=4 * slots * width**3, bytes_accessed=18 * slots * width**2, transcendentals=0
        ),
        name="gram",
    )(tiles, stat_left, stat_right)


def reduce_rows(grads, replicas, ncols):
    rows, cols = grads.shape[1] // replicas, grads.shape[2]
    parts = grads.reshape(replicas, 2, rows // 2, cols)
    me = lax.axis_index("replica")
    rightward = [(i, (i + 1) % replicas) for i in range(replicas)]
    leftward = [(i, (i - 1) % replicas) for i in range(replicas)]

    def part(shift, side):
        index = lax.rem(me + shift, replicas)
        return lax.dynamic_slice(parts, (index, side, 0, 0), (1, 1, rows // 2, cols))[0, 0]

    parts, far_right, far_left = lax.optimization_barrier((parts, part(2, 0), part(2, 1)))
    from_left = lax.ppermute(far_right, "replica", rightward)
    from_right = lax.ppermute(far_left, "replica", leftward)
    right_plain = lax.ppermute(part(1, 1), "replica", rightward)
    left_plain = lax.ppermute(part(3, 0), "replica", leftward)

    def add(first, second):
        return (first.astype(jnp.float32) + second.astype(jnp.float32)).astype(grads.dtype)

    right_sum = lax.ppermute(add(part(1, 0), from_left), "replica", rightward)
    left_sum = lax.ppermute(add(part(3, 1), from_right), "replica", leftward)
    return combine(
        jnp.reshape(me, (1,)).astype(jnp.int32),
        parts,
        right_plain,
        right_sum,
        left_plain,
        left_sum,
        ncols,
    )


def on_device(grads, block_owner, block_offsets, stat_left, stat_right, root_left, root_right):
    shards = lax.axis_size("shard")
    replicas = lax.axis_size("replica")
    devices = replicas * shards
    slots, width = stat_left.shape[:2]
    ncols = grads.shape[2] // width
    blocks = block_owner.shape[0]
    across = width // LANES
    groups = width // ROWS
    row = block_offsets[:, 0] // width
    col = block_offsets[:, 1] // width


    def owners_by(place):
        here = place[None, :] == jnp.arange(blocks, dtype=jnp.int32)[:, None]
        return jnp.sum(jnp.where(here, block_owner[None, :], 0), axis=1)

    by_source = owners_by((row ^ FAR_SHARD) * ncols + col)
    by_home = owners_by((col * shards + row) ^ FAR_DEVICE)

    summed = reduce_rows(grads, replicas, ncols)
    summed, by_source, by_home = lax.optimization_barrier((summed, by_source, by_home))
    spread = lax.all_to_all(
        summed.reshape(shards, ncols, ROWS, LANES),
        "shard",
        split_axis=0,
        concat_axis=0,
        axis_index_groups=[[index ^ FAR_SHARD for index in range(shards)]],
        tiled=True,
    )
    by_slot = to_slots(by_source, spread.reshape(blocks, ROWS, LANES), devices * slots)
    everyone = ("replica", "shard")
    owned = lax.all_to_all(
        by_slot.reshape(devices, slots, ROWS, LANES),
        everyone,
        split_axis=0,
        concat_axis=0,
        tiled=True,
    ).reshape(groups, across, slots, ROWS, LANES)
    steer = steer_slots(owned, root_left, root_right)
    new_left, new_right = gram_slots(owned, stat_left, stat_right)
    returned = lax.all_to_all(
        steer.reshape(devices, slots, ROWS, LANES),
        everyone,
        split_axis=0,
        concat_axis=0,
        tiled=True,
    )
    by_place = pick(by_home, returned.reshape(devices * slots, ROWS, LANES))
    home = lax.all_to_all(
        by_place,
        everyone,
        split_axis=0,
        concat_axis=0,
        axis_index_groups=[[index ^ FAR_DEVICE for index in range(devices)]],
        tiled=True,
    )
    direction = (
        home.reshape(groups, across, ROWS, LANES).transpose(0, 2, 1, 3).reshape(width, width)
    )
    return (new_left, new_right, direction)


def solution(mesh):
    placed = (
        P("replica", "shard", None),
        P(),
        P(),
        P(("replica", "shard"), None, None),
        P(("replica", "shard"), None, None),
        P(("replica", "shard"), None, None),
        P(("replica", "shard"), None, None),
    )
    return jax.shard_map(
        on_device,
        mesh=mesh,
        in_specs=placed,
        out_specs=(
            P(("replica", "shard"), None, None),
            P(("replica", "shard"), None, None),
            P("shard", "replica"),
        ),
        check_vma=False,
    )
```

```python
import functools

import jax
import jax.numpy as jnp
from jax import lax
from jax.experimental import pallas as pl
from jax.experimental.pallas import tpu as pltpu
from jax.sharding import PartitionSpec as P

ROWS = 8
LANES = 128
UNROLL = 32
PARTS = 4
FAR_SHARD = 41
FAR_DEVICE = 169
STRIDE = 2
VMEM_LIMIT = 16 * 1024 * 1024
GRAM_VMEM = 62 * 1024 * 1024
IN_VMEM = pl.BlockSpec(memory_space=pltpu.VMEM)
IN_SMEM = pl.BlockSpec(memory_space=pltpu.SMEM)
PARAMS = pltpu.CompilerParams(vmem_limit_bytes=VMEM_LIMIT)


def combine_kernel(ncols, me_ref, own_ref, *refs):
    out_ref = refs[-1]
    right_plain, right_sum, left_plain, left_sum = refs[:-1]
    half = right_plain.shape[0]
    across = out_ref.shape[1]
    groups = half // ROWS
    me = me_ref[0]
    for side, (first, second) in enumerate(((right_sum, left_plain), (right_plain, left_sum))):
        for block in range(ncols):
            for tile in range(across):
                lanes = pl.ds((block * across + tile) * LANES, LANES)
                total = (
                    own_ref[me, side, :, lanes].astype(jnp.float32)
                    + first[:, lanes].astype(jnp.float32)
                    + second[:, lanes].astype(jnp.float32)
                ).astype(out_ref.dtype)
                for group in range(groups):
                    row = (side * groups + group) ^ (FAR_SHARD // across)
                    out_ref[row, tile ^ (FAR_SHARD % across), block] = total[group * ROWS : (group + 1) * ROWS]


def combine(me, parts, right_plain, right_sum, left_plain, left_sum, ncols):
    half, cols = right_plain.shape
    shape = (2 * half // ROWS, cols // ncols // LANES, ncols, ROWS, LANES)
    return pl.pallas_call(
        functools.partial(combine_kernel, ncols),
        out_shape=jax.ShapeDtypeStruct(shape, parts.dtype),
        in_specs=[IN_SMEM] + [IN_VMEM] * 5,
        out_specs=IN_VMEM,
        compiler_params=PARAMS,
        name="combine",
    )(me, parts, right_plain, right_sum, left_plain, left_sum)


def to_slots_kernel(target_ref, in_ref, out_ref):
    out_ref[...] = jnp.zeros_like(out_ref)

    def step(group, carry):
        rows = [group * UNROLL + offset for offset in range(UNROLL)]
        pieces = [in_ref[row] for row in rows]
        for row, piece in zip(rows, pieces):
            out_ref[target_ref[row]] = piece
        return carry

    lax.fori_loop(0, target_ref.shape[0] // UNROLL, step, 0)


def to_slots(target, tiles, count):
    return pl.pallas_call(
        to_slots_kernel,
        out_shape=jax.ShapeDtypeStruct((count,) + tiles.shape[1:], tiles.dtype),
        in_specs=[IN_SMEM, IN_VMEM],
        out_specs=IN_VMEM,
        compiler_params=PARAMS,
        name="to_slots",
    )(target, tiles)


def pick_kernel(index_ref, in_ref, out_ref, filled, sems):
    parts = sems.shape[0]
    count = filled.shape[0] // parts

    def move(part):
        rows = pl.ds(part * count, count)
        return pltpu.make_async_copy(filled.at[rows], out_ref.at[rows], sems.at[part])

    for part in range(parts):

        def step(group, carry):
            rows = [part * count + group * UNROLL + offset for offset in range(UNROLL)]
            pieces = [in_ref[index_ref[row]] for row in rows]
            for row, piece in zip(rows, pieces):
                filled[row] = piece
            return carry

        lax.fori_loop(0, count // UNROLL, step, 0)
        move(part).start()
    for part in range(parts):
        move(part).wait()


def pick(index, tiles):
    shape = index.shape + tiles.shape[1:]
    return pl.pallas_call(
        pick_kernel,
        out_shape=jax.ShapeDtypeStruct(shape, tiles.dtype),
        in_specs=[IN_SMEM, IN_VMEM],
        out_specs=pl.BlockSpec(memory_space=pltpu.HBM),
        scratch_shapes=[pltpu.VMEM(shape, tiles.dtype), pltpu.SemaphoreType.DMA((PARTS,))],
        compiler_params=PARAMS,
        name="pick",
    )(index, tiles)


def assemble(tiles_ref, slot):
    groups, across = tiles_ref.shape[:2]
    columns = [tiles_ref[:, tile, slot].reshape(groups * ROWS, LANES) for tile in range(across)]
    return jnp.concatenate(columns, axis=1)


def steer_kernel(tiles_ref, left_ref, right_ref, out_ref):
    groups, across, slots = out_ref.shape[:3]
    for slot in range(slots):
        block = assemble(tiles_ref, slot)
        right_side = jnp.dot(block, right_ref[slot], preferred_element_type=jnp.float32)
        right_side = right_side.astype(out_ref.dtype)
        steer = jnp.dot(left_ref[slot], right_side, preferred_element_type=jnp.float32)
        steer = steer.astype(out_ref.dtype)
        for tile in range(across):
            piece = steer[:, tile * LANES : (tile + 1) * LANES].reshape(groups, ROWS, LANES)
            for group in range(0, groups, STRIDE):
                rows = pl.ds(group ^ (FAR_DEVICE // across), STRIDE)
                out_ref[rows, tile ^ (FAR_DEVICE % across), slot] = piece[group : group + STRIDE]


def gram_kernel(tiles_ref, left_ref, right_ref, new_left_ref, new_right_ref, held, in_sems, out_sems):
    slots, width = left_ref.shape[:2]

    def copies(slot):
        for side, (old, new) in enumerate(((left_ref, new_left_ref), (right_ref, new_right_ref))):
            space = held.at[slot, side]
            yield (
                pltpu.make_async_copy(old.at[slot], space, in_sems.at[slot, side]),
                pltpu.make_async_copy(space, new.at[slot], out_sems.at[slot, side]),
            )

    for slot in range(slots):
        for arriving, _ in copies(slot):
            arriving.start()
    for slot in range(slots):
        block = assemble(tiles_ref, slot)
        for side, (arriving, leaving) in enumerate(copies(slot)):
            contracted = ((1 - side,), (1 - side,))
            gram = lax.dot_general(
                block, block, (contracted, ((), ())), preferred_element_type=jnp.float32
            )
            arriving.wait()
            held[slot, side] += gram / width
            leaving.start()
    for slot in range(slots):
        for _, leaving in copies(slot):
            leaving.wait()


def steer_slots(tiles, root_left, root_right):
    slots, width = root_left.shape[:2]
    return pl.pallas_call(
        steer_kernel,
        out_shape=jax.ShapeDtypeStruct(tiles.shape, tiles.dtype),
        in_specs=[IN_VMEM] * 3,
        out_specs=IN_VMEM,
        compiler_params=PARAMS,
        cost_estimate=pl.CostEstimate(
            flops=4 * slots * width**3, bytes_accessed=8 * slots * width**2, transcendentals=0
        ),
        name="steer",
    )(tiles, root_left, root_right)


def gram_slots(tiles, stat_left, stat_right):
    slots, width = stat_left.shape[:2]
    in_hbm = pl.BlockSpec(memory_space=pltpu.HBM)
    return pl.pallas_call(
        gram_kernel,
        out_shape=[jax.ShapeDtypeStruct(stat.shape, stat.dtype) for stat in (stat_left, stat_right)],
        in_specs=[IN_VMEM, in_hbm, in_hbm],
        out_specs=[in_hbm, in_hbm],
        scratch_shapes=[
            pltpu.VMEM((slots, 2, width, width), jnp.float32),
            pltpu.SemaphoreType.DMA((slots, 2)),
            pltpu.SemaphoreType.DMA((slots, 2)),
        ],
        compiler_params=pltpu.CompilerParams(vmem_limit_bytes=GRAM_VMEM),
        cost_estimate=pl.CostEstimate(
            flops=4 * slots * width**3, bytes_accessed=18 * slots * width**2, transcendentals=0
        ),
        name="gram",
    )(tiles, stat_left, stat_right)


def reduce_rows(grads, replicas, ncols):
    rows, cols = grads.shape[1] // replicas, grads.shape[2]
    parts = grads.reshape(replicas, 2, rows // 2, cols)
    me = lax.axis_index("replica")
    rightward = [(i, (i + 1) % replicas) for i in range(replicas)]
    leftward = [(i, (i - 1) % replicas) for i in range(replicas)]

    def part(shift, side):
        index = lax.rem(me + shift, replicas)
        return lax.dynamic_slice(parts, (index, side, 0, 0), (1, 1, rows // 2, cols))[0, 0]

    parts, far_right, far_left = lax.optimization_barrier((parts, part(2, 0), part(2, 1)))
    from_left = lax.ppermute(far_right, "replica", rightward)
    from_right = lax.ppermute(far_left, "replica", leftward)
    right_plain = lax.ppermute(part(1, 1), "replica", rightward)
    left_plain = lax.ppermute(part(3, 0), "replica", leftward)

    def add(first, second):
        return (first.astype(jnp.float32) + second.astype(jnp.float32)).astype(grads.dtype)

    right_sum = lax.ppermute(add(part(1, 0), from_left), "replica", rightward)
    left_sum = lax.ppermute(add(part(3, 1), from_right), "replica", leftward)
    return combine(
        jnp.reshape(me, (1,)).astype(jnp.int32),
        parts,
        right_plain,
        right_sum,
        left_plain,
        left_sum,
        ncols,
    )


def on_device(grads, block_owner, block_offsets, stat_left, stat_right, root_left, root_right):
    shards = lax.axis_size("shard")
    replicas = lax.axis_size("replica")
    devices = replicas * shards
    slots, width = stat_left.shape[:2]
    ncols = grads.shape[2] // width
    blocks = block_owner.shape[0]
    across = width // LANES
    groups = width // ROWS
    row = block_offsets[:, 0] // width
    col = block_offsets[:, 1] // width


    def owners_by(place):
        here = place[None, :] == jnp.arange(blocks, dtype=jnp.int32)[:, None]
        return jnp.sum(jnp.where(here, block_owner[None, :], 0), axis=1)

    by_source = owners_by((row ^ FAR_SHARD) * ncols + col)
    by_home = owners_by((col * shards + row) ^ FAR_DEVICE)

    summed = reduce_rows(grads, replicas, ncols)
    summed, by_source, by_home = lax.optimization_barrier((summed, by_source, by_home))
    spread = lax.all_to_all(
        summed.reshape(shards, ncols, ROWS, LANES),
        "shard",
        split_axis=0,
        concat_axis=0,
        axis_index_groups=[[index ^ FAR_SHARD for index in range(shards)]],
        tiled=True,
    )
    by_slot = to_slots(by_source, spread.reshape(blocks, ROWS, LANES), devices * slots)
    everyone = ("replica", "shard")
    owned = lax.all_to_all(
        by_slot.reshape(devices, slots, ROWS, LANES),
        everyone,
        split_axis=0,
        concat_axis=0,
        tiled=True,
    ).reshape(groups, across, slots, ROWS, LANES)
    steer = steer_slots(owned, root_left, root_right)
    new_left, new_right = gram_slots(owned, stat_left, stat_right)
    returned = lax.all_to_all(
        steer.reshape(devices, slots, ROWS, LANES),
        everyone,
        split_axis=0,
        concat_axis=0,
        tiled=True,
    )
    by_place = pick(by_home, returned.reshape(devices * slots, ROWS, LANES))
    home = lax.all_to_all(
        by_place,
        everyone,
        split_axis=0,
        concat_axis=0,
        axis_index_groups=[[index ^ FAR_DEVICE for index in range(devices)]],
        tiled=True,
    )
    direction = (
        home.reshape(groups, across, ROWS, LANES).transpose(0, 2, 1, 3).reshape(width, width)
    )
    return (new_left, new_right, direction)


def solution(mesh):
    placed = (
        P("replica", "shard", None),
        P(),
        P(),
        P(("replica", "shard"), None, None),
        P(("replica", "shard"), None, None),
        P(("replica", "shard"), None, None),
        P(("replica", "shard"), None, None),
    )
    return jax.shard_map(
        on_device,
        mesh=mesh,
        in_specs=placed,
        out_specs=(
            P(("replica", "shard"), None, None),
            P(("replica", "shard"), None, None),
            P("shard", "replica"),
        ),
        check_vma=False,
    )
```

```python
import functools

import jax
import jax.numpy as jnp
from jax import lax
from jax.experimental import pallas as pl
from jax.experimental.pallas import tpu as pltpu
from jax.sharding import PartitionSpec as P

ROWS = 8
LANES = 128
UNROLL = 32
PARTS = 4
FAR_SHARD = 41
FAR_DEVICE = 169
STRIDE = 2
VMEM_LIMIT = 16 * 1024 * 1024
GRAM_VMEM = 62 * 1024 * 1024
IN_VMEM = pl.BlockSpec(memory_space=pltpu.VMEM)
IN_SMEM = pl.BlockSpec(memory_space=pltpu.SMEM)
PARAMS = pltpu.CompilerParams(vmem_limit_bytes=VMEM_LIMIT)


def combine_kernel(ncols, me_ref, own_ref, *refs):
    out_ref = refs[-1]
    right_plain, right_sum, left_plain, left_sum = refs[:-1]
    half = right_plain.shape[0]
    across = out_ref.shape[1]
    groups = half // ROWS
    me = me_ref[0]
    for side, (first, second) in enumerate(((right_sum, left_plain), (right_plain, left_sum))):
        for block in range(ncols):
            for tile in range(across):
                lanes = pl.ds((block * across + tile) * LANES, LANES)
                total = (
                    own_ref[me, side, :, lanes].astype(jnp.float32)
                    + first[:, lanes].astype(jnp.float32)
                    + second[:, lanes].astype(jnp.float32)
                ).astype(out_ref.dtype)
                for group in range(groups):
                    row = (side * groups + group) ^ (FAR_SHARD // across)
                    out_ref[row, tile ^ (FAR_SHARD % across), block] = total[group * ROWS : (group + 1) * ROWS]


def combine(me, parts, right_plain, right_sum, left_plain, left_sum, ncols):
    half, cols = right_plain.shape
    shape = (2 * half // ROWS, cols // ncols // LANES, ncols, ROWS, LANES)
    return pl.pallas_call(
        functools.partial(combine_kernel, ncols),
        out_shape=jax.ShapeDtypeStruct(shape, parts.dtype),
        in_specs=[IN_SMEM] + [IN_VMEM] * 5,
        out_specs=IN_VMEM,
        compiler_params=PARAMS,
        name="combine",
    )(me, parts, right_plain, right_sum, left_plain, left_sum)


def to_slots_kernel(target_ref, in_ref, out_ref):
    out_ref[...] = jnp.zeros_like(out_ref)

    def step(group, carry):
        rows = [group * UNROLL + offset for offset in range(UNROLL)]
        pieces = [in_ref[row] for row in rows]
        for row, piece in zip(rows, pieces):
            out_ref[target_ref[row]] = piece
        return carry

    lax.fori_loop(0, target_ref.shape[0] // UNROLL, step, 0)


def to_slots(target, tiles, count):
    return pl.pallas_call(
        to_slots_kernel,
        out_shape=jax.ShapeDtypeStruct((count,) + tiles.shape[1:], tiles.dtype),
        in_specs=[IN_SMEM, IN_VMEM],
        out_specs=IN_VMEM,
        compiler_params=PARAMS,
        name="to_slots",
    )(target, tiles)


def pick_kernel(index_ref, in_ref, out_ref, filled, sems):
    parts = sems.shape[0]
    count = filled.shape[0] // parts

    def move(part):
        rows = pl.ds(part * count, count)
        return pltpu.make_async_copy(filled.at[rows], out_ref.at[rows], sems.at[part])

    for part in range(parts):

        def step(group, carry):
            rows = [part * count + group * UNROLL + offset for offset in range(UNROLL)]
            pieces = [in_ref[index_ref[row]] for row in rows]
            for row, piece in zip(rows, pieces):
                filled[row] = piece
            return carry

        lax.fori_loop(0, count // UNROLL, step, 0)
        move(part).start()
    for part in range(parts):
        move(part).wait()


def pick(index, tiles):
    shape = index.shape + tiles.shape[1:]
    return pl.pallas_call(
        pick_kernel,
        out_shape=jax.ShapeDtypeStruct(shape, tiles.dtype),
        in_specs=[IN_SMEM, IN_VMEM],
        out_specs=pl.BlockSpec(memory_space=pltpu.HBM),
        scratch_shapes=[pltpu.VMEM(shape, tiles.dtype), pltpu.SemaphoreType.DMA((PARTS,))],
        compiler_params=PARAMS,
        name="pick",
    )(index, tiles)


def assemble(tiles_ref, slot):
    groups, across = tiles_ref.shape[:2]
    columns = [tiles_ref[:, tile, slot].reshape(groups * ROWS, LANES) for tile in range(across)]
    return jnp.concatenate(columns, axis=1)


def steer_kernel(tiles_ref, left_ref, right_ref, out_ref):
    groups, across, slots = out_ref.shape[:3]
    for slot in range(slots):
        block = assemble(tiles_ref, slot)
        right_side = jnp.dot(block, right_ref[slot], preferred_element_type=jnp.float32)
        right_side = right_side.astype(out_ref.dtype)
        steer = jnp.dot(left_ref[slot], right_side, preferred_element_type=jnp.float32)
        steer = steer.astype(out_ref.dtype)
        for tile in range(across):
            piece = steer[:, tile * LANES : (tile + 1) * LANES].reshape(groups, ROWS, LANES)
            for group in range(0, groups, STRIDE):
                rows = pl.ds(group ^ (FAR_DEVICE // across), STRIDE)
                out_ref[rows, tile ^ (FAR_DEVICE % across), slot] = piece[group : group + STRIDE]


def gram_kernel(tiles_ref, left_ref, right_ref, new_left_ref, new_right_ref, held, in_sems, out_sems):
    slots, width = left_ref.shape[:2]

    def copies(slot):
        for side, (old, new) in enumerate(((left_ref, new_left_ref), (right_ref, new_right_ref))):
            space = held.at[slot, side]
            yield (
                pltpu.make_async_copy(old.at[slot], space, in_sems.at[slot, side]),
                pltpu.make_async_copy(space, new.at[slot], out_sems.at[slot, side]),
            )

    for slot in range(slots):
        for arriving, _ in copies(slot):
            arriving.start()
    for slot in range(slots):
        block = assemble(tiles_ref, slot)
        for side, (arriving, leaving) in enumerate(copies(slot)):
            contracted = ((1 - side,), (1 - side,))
            gram = lax.dot_general(
                block, block, (contracted, ((), ())), preferred_element_type=jnp.float32
            )
            arriving.wait()
            held[slot, side] += gram / width
            leaving.start()
    for slot in range(slots):
        for _, leaving in copies(slot):
            leaving.wait()


def steer_slots(tiles, root_left, root_right):
    slots, width = root_left.shape[:2]
    return pl.pallas_call(
        steer_kernel,
        out_shape=jax.ShapeDtypeStruct(tiles.shape, tiles.dtype),
        in_specs=[IN_VMEM] * 3,
        out_specs=IN_VMEM,
        compiler_params=PARAMS,
        cost_estimate=pl.CostEstimate(
            flops=4 * slots * width**3, bytes_accessed=8 * slots * width**2, transcendentals=0
        ),
        name="steer",
    )(tiles, root_left, root_right)


def gram_slots(tiles, stat_left, stat_right):
    slots, width = stat_left.shape[:2]
    in_hbm = pl.BlockSpec(memory_space=pltpu.HBM)
    return pl.pallas_call(
        gram_kernel,
        out_shape=[jax.ShapeDtypeStruct(stat.shape, stat.dtype) for stat in (stat_left, stat_right)],
        in_specs=[IN_VMEM, in_hbm, in_hbm],
        out_specs=[in_hbm, in_hbm],
        scratch_shapes=[
            pltpu.VMEM((slots, 2, width, width), jnp.float32),
            pltpu.SemaphoreType.DMA((slots, 2)),
            pltpu.SemaphoreType.DMA((slots, 2)),
        ],
        compiler_params=pltpu.CompilerParams(vmem_limit_bytes=GRAM_VMEM),
        cost_estimate=pl.CostEstimate(
            flops=4 * slots * width**3, bytes_accessed=18 * slots * width**2, transcendentals=0
        ),
        name="gram",
    )(tiles, stat_left, stat_right)


def reduce_rows(grads, replicas, ncols):
    rows, cols = grads.shape[1] // replicas, grads.shape[2]
    parts = grads.reshape(replicas, 2, rows // 2, cols)
    me = lax.axis_index("replica")
    rightward = [(i, (i + 1) % replicas) for i in range(replicas)]
    leftward = [(i, (i - 1) % replicas) for i in range(replicas)]

    def part(shift, side, parts):
        index = lax.rem(me + shift, replicas)
        return lax.dynamic_slice(parts, (index, side, 0, 0), (1, 1, rows // 2, cols))[0, 0]

    parts, far_right, far_left = lax.optimization_barrier(
        (parts, part(2, 0, parts), part(2, 1, parts))
    )
    from_left = lax.ppermute(far_right, "replica", rightward)
    from_right = lax.ppermute(far_left, "replica", leftward)
    right_plain = lax.ppermute(part(1, 1, parts), "replica", rightward)
    left_plain = lax.ppermute(part(3, 0, parts), "replica", leftward)

    def add(first, second):
        return (first.astype(jnp.float32) + second.astype(jnp.float32)).astype(grads.dtype)

    own, from_left = lax.optimization_barrier((parts, from_left))
    right_sum = lax.ppermute(add(part(1, 0, own), from_left), "replica", rightward)
    own, from_right = lax.optimization_barrier((parts, from_right))
    left_sum = lax.ppermute(add(part(3, 1, own), from_right), "replica", leftward)
    return combine(
        jnp.reshape(me, (1,)).astype(jnp.int32),
        parts,
        right_plain,
        right_sum,
        left_plain,
        left_sum,
        ncols,
    )


def on_device(grads, block_owner, block_offsets, stat_left, stat_right, root_left, root_right):
    shards = lax.axis_size("shard")
    replicas = lax.axis_size("replica")
    devices = replicas * shards
    slots, width = stat_left.shape[:2]
    ncols = grads.shape[2] // width
    blocks = block_owner.shape[0]
    across = width // LANES
    groups = width // ROWS
    row = block_offsets[:, 0] // width
    col = block_offsets[:, 1] // width

    def owners_by(place):
        here = place[None, :] == jnp.arange(blocks, dtype=jnp.int32)[:, None]
        return jnp.sum(jnp.where(here, block_owner[None, :], 0), axis=1)

    by_source = owners_by((row ^ FAR_SHARD) * ncols + col)
    by_home = owners_by((col * shards + row) ^ FAR_DEVICE)

    summed = reduce_rows(grads, replicas, ncols)
    summed, by_source, by_home = lax.optimization_barrier((summed, by_source, by_home))
    spread = lax.all_to_all(
        summed.reshape(shards, ncols, ROWS, LANES),
        "shard",
        split_axis=0,
        concat_axis=0,
        axis_index_groups=[[index ^ FAR_SHARD for index in range(shards)]],
        tiled=True,
    )
    by_slot = to_slots(by_source, spread.reshape(blocks, ROWS, LANES), devices * slots)
    everyone = ("replica", "shard")
    owned = lax.all_to_all(
        by_slot.reshape(devices, slots, ROWS, LANES),
        everyone,
        split_axis=0,
        concat_axis=0,
        tiled=True,
    ).reshape(groups, across, slots, ROWS, LANES)
    steer = steer_slots(owned, root_left, root_right)
    new_left, new_right = gram_slots(owned, stat_left, stat_right)
    returned = lax.all_to_all(
        steer.reshape(devices, slots, ROWS, LANES),
        everyone,
        split_axis=0,
        concat_axis=0,
        tiled=True,
    )
    by_place = pick(by_home, returned.reshape(devices * slots, ROWS, LANES))
    home = lax.all_to_all(
        by_place,
        everyone,
        split_axis=0,
        concat_axis=0,
        axis_index_groups=[[index ^ FAR_DEVICE for index in range(devices)]],
        tiled=True,
    )
    direction = (
        home.reshape(groups, across, ROWS, LANES).transpose(0, 2, 1, 3).reshape(width, width)
    )
    return (new_left, new_right, direction)


def solution(mesh):
    placed = (
        P("replica", "shard", None),
        P(),
        P(),
        P(("replica", "shard"), None, None),
        P(("replica", "shard"), None, None),
        P(("replica", "shard"), None, None),
        P(("replica", "shard"), None, None),
    )
    return jax.shard_map(
        on_device,
        mesh=mesh,
        in_specs=placed,
        out_specs=(
            P(("replica", "shard"), None, None),
            P(("replica", "shard"), None, None),
            P("shard", "replica"),
        ),
        check_vma=False,
    )
```
